32 devices in a mesh: lat: 4 (over z), lon: 2 (over x), chan: 4 (over y, core).
Axes of the slice: x: 2, y: 2, z: 4, core: 2. Of those that a mesh axis runs over, the one named last changes fastest.
Arguments:
- queries: bfloat16 [64, 16, 2560], P('lat', 'lon', 'chan'), may hold values from -8 to 8
- keys: bfloat16 [64, 16, 2560], P('lat', 'lon', 'chan'), may hold values from -8 to 8
- values: bfloat16 [64, 16, 2560], P('lat', 'lon', 'chan'), may hold values from -6 to 6
- attn_out: bfloat16 [64, 16, 2560], P('lat', 'lon', 'chan'), may hold values from -6 to 6
- grad_out: bfloat16 [64, 16, 5120], P('lat', 'lon', 'chan'), may hold values from -6 to 6
- w_out: bfloat16 [5120, 2560], P(('lat', 'lon'), 'chan'), may hold values from -0.078125 to 0.078125
- bias_table: float32 [20, 25, 13], P('chan'), may hold values from -5 to 5
- key_mask: int32 [64, 16], replicated, may hold values 0 or 1
Outputs:
- grad_queries: bfloat16 [64, 16, 2560], P('lat', 'lon', 'chan')
- grad_keys: bfloat16 [64, 16, 2560], P('lat', 'lon', 'chan')
- grad_values: bfloat16 [64, 16, 2560], P('lat', 'lon', 'chan')
- grad_wout: float32 [5120, 2560], P(('lat', 'lon'), 'chan')
- grad_table: float32 [20, 25, 13], P('chan')
The draws below stay inside these ranges and needn't reach their ends.
All inputs are finite; a program needn't handle non-finite values.
Results may differ from the reference program's by a relative error of at most 0.007.
Values may be sent and summed in bfloat16 or wider, within the bound.
A program may use at most 128 MiB of HBM per device.

```python
import jax
import jax.numpy as jnp
from jax import lax

D = 5120
HEADS = 20
HEAD_DIM = 128
WIN = 13
LAT_ALL = 64
LON_ALL = 16


def draw_pair(key):
    dims_all = (LAT_ALL, LON_ALL, HEADS * HEAD_DIM)
    query_draw = jnp.clip(jax.random.normal(jax.random.fold_in(key, 21), dims_all, jnp.float32), -6.0, 6.0)
    key_draw = jnp.clip(jax.random.normal(jax.random.fold_in(key, 22), dims_all, jnp.float32), -6.0, 6.0)
    return (query_draw, key_draw)


def draw_queries(key, part):
    return draw_pair(key)[0].astype(jnp.bfloat16)


def draw_keys(key, part):
    return draw_pair(key)[1].astype(jnp.bfloat16)


def plant(drawn, own_key, least, top_value):
    place = [jax.random.randint(jax.random.fold_in(own_key, axis), (), 0, length) for axis, length in enumerate(drawn.shape)]
    main_axis = drawn.shape.index(max(drawn.shape))
    neighbour = place[:main_axis] + [(place[main_axis] + 1) % drawn.shape[main_axis]] + place[main_axis + 1:]
    return drawn.at[tuple(place)].set(least).at[tuple(neighbour)].set(top_value)


def steps_of(own_key, extent, pieces, smallest, high):
    factor_of, own = 1.0, jax.random.fold_in(own_key, 6)
    for position, parts in pieces:
        steps = jnp.exp(jax.random.uniform(jax.random.fold_in(own, position), (parts,), jnp.float32, smallest / len(pieces), high / len(pieces)))
        factor_of = factor_of * jnp.repeat(steps, extent[position] // parts).reshape([-1 if axis == position else 1 for axis in range(len(extent))])
    return factor_of


def noise(rng, dims, spread, most, split=(), held_as=jnp.bfloat16):
    factor_of = steps_of(rng, dims, split, -0.22, 0.18) if split else 1.0
    entries = jax.random.normal(rng, dims, jnp.float32) * spread * factor_of
    return jnp.minimum(jnp.maximum(entries, -most), most).astype(held_as)


def setup_inputs(seed: int = 0) -> dict:
    splits = jax.random.split(jax.random.key(seed), 9)
    return {
        "queries": draw_queries(jax.random.fold_in(splits[8], 71), 0),
        "keys": draw_keys(jax.random.fold_in(splits[8], 71), 0),
        "values": noise(splits[2], (LAT_ALL, LON_ALL, HEADS * HEAD_DIM), 1.0, 6.0, ((0, 4), (1, 2), (2, 4))),
        "attn_out": noise(splits[3], (LAT_ALL, LON_ALL, HEADS * HEAD_DIM), 1.0, 6.0, ((0, 4), (1, 2), (2, 4))),
        "grad_out": noise(splits[4], (LAT_ALL, LON_ALL, D), 1.0, 6.0, ((0, 4), (1, 2), (2, 4))),
        "w_out": noise(splits[5], (D, HEADS * HEAD_DIM), D ** -0.5, 0.078125, ((0, 8), (1, 4))),
        "bias_table": noise(splits[6], (HEADS, 2 * WIN - 1, WIN), 1.0, 5.0, ((0, 4),), jnp.float32),
        "key_mask": plant((jax.random.randint(splits[7], (LAT_ALL, LON_ALL), 0, 4) < 3).astype(jnp.int32), jax.random.fold_in(splits[7], 1), 0, 1),
    }


def reference(queries, keys, values, attn_out, grad_out, w_out, bias_table, key_mask):
    lat_total, lon_total, chan_width = queries.shape
    head_count = bias_table.shape[0]
    reach_cells = WIN // 2
    score_scale = HEAD_DIM ** -0.5
    token_count = lat_total * lon_total
    flat_grad = grad_out.reshape(token_count, -1)
    grad_attn = jnp.dot(flat_grad, w_out, preferred_element_type=jnp.float32).astype(jnp.bfloat16)
    grad_attn = grad_attn.reshape(lat_total, lon_total, head_count, HEAD_DIM)
    grad_wout = lax.dot_general(flat_grad, attn_out.reshape(token_count, chan_width), (((0,), (0,)), ((), ())), preferred_element_type=jnp.float32)
    lat_index = jnp.arange(lat_total, dtype=jnp.int32)
    lon_index = jnp.arange(lon_total, dtype=jnp.int32)
    valid_keys = (key_mask == 1) | ((lat_index % 4 == 0)[:, None] & (lon_index % 4 == 0)[None, :])
    pick_cols = ((lon_index[:, None] + jnp.arange(WIN, dtype=jnp.int32)[None, :] - reach_cells) % lon_total).astype(jnp.int32)
    query_heads = queries.reshape(lat_total, lon_total, head_count, HEAD_DIM)
    key_heads = keys.reshape(lat_total, lon_total, head_count, HEAD_DIM)
    value_heads = values.reshape(lat_total, lon_total, head_count, HEAD_DIM)

    def row_step(state_sum, row_index):
        grad_k, grad_v, grad_tab = state_sum
        first_row = jnp.clip(row_index - reach_cells, 0, lat_total - WIN).astype(jnp.int32)
        key_rows = lax.dynamic_slice_in_dim(key_heads, first_row, WIN, 0).astype(jnp.float32)
        value_rows = lax.dynamic_slice_in_dim(value_heads, first_row, WIN, 0).astype(jnp.float32)
        key_pick = key_rows[:, pick_cols]
        value_pick = value_rows[:, pick_cols]
        query_h = lax.dynamic_index_in_dim(query_heads, row_index, 0, keepdims=False).astype(jnp.float32)
        grad_row = lax.dynamic_index_in_dim(grad_attn, row_index, 0, keepdims=False).astype(jnp.float32)
        key_ok = lax.dynamic_slice_in_dim(valid_keys, first_row, WIN, 0)[:, pick_cols]
        allowed = key_ok.transpose(1, 0, 2)
        table_first = (first_row - row_index + WIN - 1).astype(jnp.int32)
        table_rows = lax.dynamic_slice_in_dim(bias_table, table_first, WIN, 1)
        scores = score_scale * jnp.einsum('chd,xckhd->hcxk', query_h, key_pick) + table_rows[:, None]
        scores = jnp.where(allowed[None], scores, -1e30)
        row_max = jnp.max(scores, axis=(2, 3), keepdims=True)
        weights_exp = jnp.exp(scores - row_max)
        prob_rows = weights_exp / jnp.sum(weights_exp, axis=(2, 3), keepdims=True)
        grad_prob = jnp.einsum('chd,xckhd->hcxk', grad_row, value_pick)
        row_delta = jnp.sum(prob_rows * grad_prob, axis=(2, 3), keepdims=True)
        dscore = prob_rows * (grad_prob - row_delta)
        table_part = jnp.sum(dscore, axis=1)
        prior_sum = lax.dynamic_slice_in_dim(grad_tab, table_first, WIN, 1)
        grad_tab = lax.dynamic_update_slice_in_dim(grad_tab, prior_sum + table_part, table_first, 1)
        dscore_low = lax.optimization_barrier(dscore.astype(jnp.bfloat16)).astype(jnp.float32)
        prob_low = lax.optimization_barrier(prob_rows.astype(jnp.bfloat16)).astype(jnp.float32)
        grad_query = (score_scale * jnp.einsum('hcxk,xckhd->chd', dscore_low, key_pick)).astype(jnp.bfloat16)
        key_part = score_scale * jnp.einsum('hcxk,chd->xckhd', dscore_low, query_h)
        value_part = jnp.einsum('hcxk,chd->xckhd', prob_low, grad_row)
        zero_rows = jnp.zeros((WIN, lon_total, head_count, HEAD_DIM), jnp.float32)
        key_add = zero_rows.at[:, pick_cols].add(key_part)
        value_add = zero_rows.at[:, pick_cols].add(value_part)
        prior_k = lax.dynamic_slice_in_dim(grad_k, first_row, WIN, 0)
        grad_k = lax.dynamic_update_slice_in_dim(grad_k, prior_k + key_add, first_row, 0)
        prior_v = lax.dynamic_slice_in_dim(grad_v, first_row, WIN, 0)
        grad_v = lax.dynamic_update_slice_in_dim(grad_v, prior_v + value_add, first_row, 0)
        return (grad_k, grad_v, grad_tab), grad_query

    zero_field = jnp.zeros((lat_total, lon_total, head_count, HEAD_DIM), jnp.float32)
    start_state = (zero_field, zero_field, jnp.zeros((head_count, 2 * WIN - 1, WIN), jnp.float32))
    (sum_k, sum_v, grad_table), grad_rows = lax.scan(row_step, start_state, lat_index)
    grad_queries = grad_rows.reshape(lat_total, lon_total, chan_width)
    grad_keys = sum_k.astype(jnp.bfloat16).reshape(lat_total, lon_total, chan_width)
    grad_values = sum_v.astype(jnp.bfloat16).reshape(lat_total, lon_total, chan_width)
    return (grad_queries, grad_keys, grad_values, grad_wout, grad_table)
```

```python
import functools

import jax
import jax.numpy as jnp
from jax import lax
from jax.experimental import pallas as pl
from jax.experimental.pallas import tpu as pltpu
from jax.sharding import PartitionSpec as P

HEAD_DIM = 128
WIN = 13
REACH = WIN // 2
SCALE = HEAD_DIM ** (-0.5)
F32 = jnp.float32
BF16 = jnp.bfloat16


def row_slots(rows, cols):
    slots = max(rows + 2 * REACH, 2 * WIN - 1)
    while slots * cols % 128:
        slots += 1
    return slots


def column_pick(cols, slots):
    wide, tight = slots * 2 * cols, slots * cols
    source = lax.broadcasted_iota(jnp.int32, (wide, tight), 0)
    lane = lax.broadcasted_iota(jnp.int32, (wide, tight), 1)
    return (source == lane // cols * (2 * cols) + lane % cols).astype(F32)


def skew(value, cols, left):
    lanes = value.shape[1]
    place = lax.broadcasted_iota(jnp.int32, value.shape, 0) % cols
    step = 1
    while step < cols:
        moved = pltpu.roll(value, lanes - step if left else step, 1)
        value = jnp.where(place // step % 2 == 1, moved, value)
        step *= 2
    return value


def expand_bias(diag, cols, slots):
    lanes = diag.shape[1]
    rows = [jnp.broadcast_to(diag[i : i + 1], (cols, lanes)) for i in range(diag.shape[0])]
    wide = pltpu.roll(jnp.concatenate(rows, axis=0), lanes - (cols - 1), 1)
    wide = skew(wide, cols, False)
    return jnp.dot(
        wide, column_pick(cols, slots), precision=lax.Precision.HIGHEST, preferred_element_type=F32
    )


def collapse_bias(spread, cols, slots):
    wide = lax.dot_general(
        spread,
        column_pick(cols, slots),
        (((1,), (1,)), ((), ())),
        precision=lax.Precision.HIGHEST,
        preferred_element_type=F32,
    )
    wide = skew(pltpu.roll(wide, cols - 1, 1), cols, True)
    return jnp.sum(wide.reshape(-1, cols, wide.shape[1]), axis=1)


def allowed_pairs(valid, lat_first, lat_total, rows, cols, slots, blocks, lon_size):
    shape = (rows * cols, blocks * slots * cols)
    query = lax.broadcasted_iota(jnp.int32, shape, 0)
    lane = lax.broadcasted_iota(jnp.int32, shape, 1)
    block = lane // (slots * cols)
    key = lane % (slots * cols)
    row = lat_first + query // cols
    first = jnp.clip(row - REACH, 0, lat_total - WIN)
    key_row = lat_first - REACH + key // cols
    delta = key % cols - query % cols
    in_lat = (key_row >= first) & (key_row < first + WIN)
    near = (delta >= -REACH) & (delta <= REACH)
    right = delta + cols <= REACH
    left = delta - cols >= -REACH
    if blocks == 1:
        in_lon = near
    elif lon_size == 2:
        in_lon = ((block == 0) & near) | ((block == 1) & (right | left))
    else:
        in_lon = ((block == 0) & near) | ((block == 1) & right) | ((block == 2) & left)
    return in_lat & in_lon & (valid > 0)


def attend(dims, allowed, spread, q, g, k, v):
    rows, cols, slots, blocks = dims
    span = slots * cols
    nt = (((1,), (1,)), ((), ()))
    tn = (((0,), (0,)), ((), ()))
    shifts = [((i - REACH) * cols) % span for i in range(rows)]
    bias = jnp.concatenate(
        [
            jnp.concatenate([pltpu.roll(part, s, 1) if s else part for s in shifts], axis=0)
            for part in (spread[b * cols : (b + 1) * cols] for b in range(blocks))
        ],
        axis=1,
    )
    scores = SCALE * lax.dot_general(q, k, nt, preferred_element_type=F32) + bias
    scores = jnp.where(allowed, scores, -1e30)
    weights = jnp.exp(scores - jnp.max(scores, axis=1, keepdims=True))
    probs = weights / jnp.sum(weights, axis=1, keepdims=True)
    grad_prob = lax.dot_general(g, v, nt, preferred_element_type=F32)
    grad_prob = jnp.where(allowed, grad_prob, 0.0)
    delta = jnp.sum(probs * grad_prob, axis=1, keepdims=True)
    dscore = probs * (grad_prob - delta)
    folded = []
    for b in range(blocks):
        total = None
        for i, s in enumerate(shifts):
            part = dscore[i * cols : (i + 1) * cols, b * span : (b + 1) * span]
            part = pltpu.roll(part, (span - s) % span, 1) if s else part
            total = part if total is None else total + part
        folded.append(total)
    low = dscore.astype(BF16)
    prob_low = probs.astype(BF16)
    grad_q = SCALE * jnp.dot(low, k, preferred_element_type=F32)
    grad_k = SCALE * lax.dot_general(low, q, tn, preferred_element_type=F32)
    grad_v = lax.dot_general(prob_low, g, tn, preferred_element_type=F32)
    return grad_q, grad_k, grad_v, folded


def attention_kernel(dims, lon_size, lat_size, valid, diag, q, g, kv, gq, gkv, table, pairs, fold):
    rows, cols, slots, blocks = dims
    lat_first = lax.axis_index("lat") * rows
    heads = q.shape[1] // HEAD_DIM
    allowed = allowed_pairs(
        valid[...], lat_first, lat_size * rows, rows, cols, slots, blocks, lon_size
    )
    spread = expand_bias(diag[...], cols, slots)
    for h in range(heads):
        at = pl.ds(h * HEAD_DIM, HEAD_DIM)
        own = spread[h * blocks * cols : (h + 1) * blocks * cols]
        grad_q, grad_k, grad_v, folded = attend(
            dims, allowed, own, q[:, at], g[:, at], kv[0, :, at], kv[1, :, at]
        )
        gq[:, at] = grad_q.astype(BF16)
        gkv[0, :, at] = grad_k
        gkv[1, :, at] = grad_v
        for b in range(blocks):
            fold[pl.ds((h * blocks + b) * cols, cols), :] = folded[b]
    table[...] = collapse_bias(fold[...], cols, slots)


def diag_table(table, cols, slots, blocks, lon_size):
    heads, height, width = table.shape

    def placed(part, first):
        return jnp.pad(part, ((0, 0), (0, 0), (first, 2 * cols - first - part.shape[2])))

    own = placed(table, cols - 1 - REACH)
    right = placed(table[:, :, REACH + 1 :], 0) if blocks > 1 else None
    left = placed(table[:, :, :REACH], 2 * cols - 1 - REACH) if blocks > 1 else None
    parts = [own] if blocks == 1 else [own, right + left] if lon_size == 2 else [own, right, left]
    stacked = jnp.stack(parts, axis=1)
    stacked = jnp.pad(stacked, ((0, 0), (0, 0), (0, slots - height), (0, 0)))
    return stacked.reshape(heads * blocks, slots * 2 * cols)


def undiag_table(diag, heads, cols, slots, blocks, lon_size):
    grid = diag.reshape(heads, blocks, slots, 2 * cols)[:, :, : 2 * WIN - 1]
    first = cols - 1 - REACH
    own = grid[:, 0, :, first : first + WIN]
    if blocks == 1:
        return own
    right = grid[:, 1, :, :REACH]
    left = grid[:, blocks - 1, :, 2 * cols - 1 - REACH : 2 * cols - 1]
    gap = jnp.zeros(own.shape[:2] + (1,), own.dtype)
    return own + jnp.concatenate([left, gap, right], axis=2)


def valid_row(key_mask, rows, cols, slots, blocks, lon_size):
    lat_total, lon_total = key_mask.shape
    mark = (jnp.arange(lat_total) % 4 == 0)[:, None] & (jnp.arange(lon_total) % 4 == 0)[None, :]
    valid = ((key_mask == 1) | mark).astype(jnp.int32)
    valid = jnp.pad(valid, ((REACH, slots), (0, 0)))
    valid = lax.dynamic_slice_in_dim(valid, lax.axis_index("lat") * rows, slots, 0)
    me = lax.axis_index("lon")
    parts = [
        lax.dynamic_slice_in_dim(valid, (me + step) % lon_size * cols, cols, 1)
        for step in (0, 1, lon_size - 1)[:blocks]
    ]
    return jnp.stack(parts, axis=0).reshape(1, blocks * slots * cols)


def local(queries, keys, values, attn_out, grad_out, w_out, bias_table, key_mask):
    rows, cols, width = queries.shape
    heads = bias_table.shape[0]
    tokens = rows * cols
    lat_size, lon_size = lax.axis_size("lat"), lax.axis_size("lon")
    blocks = min(3, lon_size)
    slots = row_slots(rows, cols)
    span = slots * cols
    rim = REACH * cols
    group = ("lat", "lon")
    dims = (rows, cols, slots, blocks)
    whole = lax.all_gather(grad_out.reshape(tokens, -1), "chan", axis=1, tiled=True)
    features = lax.all_to_all(whole, group, split_axis=1, concat_axis=0, tiled=True)
    part = jnp.dot(features, w_out, preferred_element_type=F32).astype(BF16)
    back = lax.all_to_all(part, group, split_axis=0, concat_axis=0, tiled=True)
    grad_attn = jnp.sum(back.reshape(-1, tokens, width).astype(F32), axis=0).astype(BF16)

    kv = jnp.stack([keys, values]).reshape(2, 1, tokens, width)
    rights = [(i, (i + 1) % lon_size) for i in range(lon_size)]
    lefts = [(j, i) for i, j in rights]
    sides = [kv]
    if blocks > 1:
        sides.append(lax.ppermute(kv, "lon", lefts))
    if blocks > 2:
        sides.append(lax.ppermute(kv, "lon", rights))
    kv = jnp.concatenate(sides, axis=1)
    up = [(i, i + 1) for i in range(lat_size - 1)]
    down = [(j, i) for i, j in up]
    before = lax.ppermute(kv[:, :, tokens - rim :], "lat", up)
    after = lax.ppermute(kv[:, :, :rim], "lat", down)
    pad = jnp.zeros((2, blocks, span - tokens - 2 * rim, width), BF16)
    kv = jnp.concatenate([before, kv, after, pad], axis=2).reshape(2, blocks * span, width)

    diag = diag_table(bias_table, cols, slots, blocks, lon_size)
    valid = valid_row(key_mask, rows, cols, slots, blocks, lon_size)
    vmem = pl.BlockSpec(memory_space=pltpu.VMEM)
    grad_queries, grad_kv, diag_grad = pl.pallas_call(
        functools.partial(attention_kernel, dims, lon_size, lat_size),
        out_shape=(
            jax.ShapeDtypeStruct((tokens, width), BF16),
            jax.ShapeDtypeStruct((2, blocks * span, width), F32),
            jax.ShapeDtypeStruct((heads * blocks, slots * 2 * cols), F32),
        ),
        in_specs=[vmem] * 5,
        out_specs=(vmem,) * 3,
        scratch_shapes=[
            pltpu.VMEM((8, 128), F32),
            pltpu.VMEM((heads * blocks * cols, span), F32),
        ],
        compiler_params=pltpu.CompilerParams(vmem_limit_bytes=40 * 1024 * 1024),
    )(valid, diag, queries.reshape(tokens, width), grad_attn, kv)

    grad_kv = grad_kv.reshape(2, blocks, span, width)
    own_before = lax.ppermute(grad_kv[:, :, :rim].astype(BF16), "lat", down).astype(F32)
    own_after = lax.ppermute(
        grad_kv[:, :, rim + tokens : 2 * rim + tokens].astype(BF16), "lat", up
    ).astype(F32)
    middle = grad_kv[:, :, rim : rim + tokens]
    middle = (
        middle
        + jnp.pad(own_before, ((0, 0), (0, 0), (tokens - rim, 0), (0, 0)))
        + jnp.pad(own_after, ((0, 0), (0, 0), (0, tokens - rim), (0, 0)))
    )
    total = middle[:, 0]
    if blocks > 1:
        total = total + lax.ppermute(middle[:, 1].astype(BF16), "lon", rights).astype(F32)
    if blocks > 2:
        total = total + lax.ppermute(middle[:, 2].astype(BF16), "lon", lefts).astype(F32)
    total = total.astype(BF16).reshape(2, rows, cols, width)
    diag_grad = lax.psum(diag_grad, group)
    grad_table = undiag_table(diag_grad, heads, cols, slots, blocks, lon_size)
    saved = lax.all_gather(attn_out.reshape(tokens, width), group, axis=0, tiled=True)
    grad_wout = lax.dot_general(
        features, saved, (((0,), (0,)), ((), ())), preferred_element_type=F32
    )
    return (grad_queries.reshape(rows, cols, width), total[0], total[1], grad_wout, grad_table)


def solution(mesh):
    token = P("lat", "lon", "chan")
    matrix = P(("lat", "lon"), "chan")
    table = P("chan", None, None)
    return jax.shard_map(
        local,
        mesh=mesh,
        in_specs=(token, token, token, token, token, matrix, table, P()),
        out_specs=(token, token, token, matrix, table),
        check_vma=False,
    )
```

```python
import functools

import jax
import jax.numpy as jnp
from jax import lax
from jax.experimental import pallas as pl
from jax.experimental.pallas import tpu as pltpu
from jax.sharding import PartitionSpec as P

HEAD_DIM = 128
WIN = 13
REACH = WIN // 2
SCALE = HEAD_DIM ** (-0.5)
F32 = jnp.float32
BF16 = jnp.bfloat16


def row_slots(rows, cols):
    slots = max(rows + 2 * REACH, 2 * WIN - 1)
    while slots * cols % 128:
        slots += 1
    return slots


def column_pick(cols, slots):
    wide, tight = slots * 2 * cols, slots * cols
    source = lax.broadcasted_iota(jnp.int32, (wide, tight), 0)
    lane = lax.broadcasted_iota(jnp.int32, (wide, tight), 1)
    return (source == lane // cols * (2 * cols) + lane % cols).astype(F32)


def skew(value, cols, left):
    lanes = value.shape[1]
    place = lax.broadcasted_iota(jnp.int32, value.shape, 0) % cols
    step = 1
    while step < cols:
        moved = pltpu.roll(value, lanes - step if left else step, 1)
        value = jnp.where(place // step % 2 == 1, moved, value)
        step *= 2
    return value


def expand_bias(diag, cols, slots):
    lanes = diag.shape[1]
    rows = [jnp.broadcast_to(diag[i : i + 1], (cols, lanes)) for i in range(diag.shape[0])]
    wide = pltpu.roll(jnp.concatenate(rows, axis=0), lanes - (cols - 1), 1)
    wide = skew(wide, cols, False)
    return jnp.dot(
        wide, column_pick(cols, slots), precision=lax.Precision.HIGHEST, preferred_element_type=F32
    )


def collapse_bias(spread, cols, slots):
    wide = lax.dot_general(
        spread,
        column_pick(cols, slots),
        (((1,), (1,)), ((), ())),
        precision=lax.Precision.HIGHEST,
        preferred_element_type=F32,
    )
    wide = skew(pltpu.roll(wide, cols - 1, 1), cols, True)
    return jnp.sum(wide.reshape(-1, cols, wide.shape[1]), axis=1)


def allowed_pairs(valid, lat_first, lat_total, rows, cols, slots, blocks, lon_size):
    shape = (rows * cols, blocks * slots * cols)
    query = lax.broadcasted_iota(jnp.int32, shape, 0)
    lane = lax.broadcasted_iota(jnp.int32, shape, 1)
    block = lane // (slots * cols)
    key = lane % (slots * cols)
    row = lat_first + query // cols
    first = jnp.clip(row - REACH, 0, lat_total - WIN)
    key_row = lat_first - REACH + key // cols
    delta = key % cols - query % cols
    in_lat = (key_row >= first) & (key_row < first + WIN)
    near = (delta >= -REACH) & (delta <= REACH)
    right = delta + cols <= REACH
    left = delta - cols >= -REACH
    if blocks == 1:
        in_lon = near
    elif lon_size == 2:
        in_lon = ((block == 0) & near) | ((block == 1) & (right | left))
    else:
        in_lon = ((block == 0) & near) | ((block == 1) & right) | ((block == 2) & left)
    return in_lat & in_lon & (valid > 0)


def attend(dims, allowed, spread, q, g, k, v):
    rows, cols, slots, blocks = dims
    span = slots * cols
    nt = (((1,), (1,)), ((), ()))
    tn = (((0,), (0,)), ((), ()))
    shifts = [((i - REACH) * cols) % span for i in range(rows)]
    bias = jnp.concatenate(
        [
            jnp.concatenate([pltpu.roll(part, s, 1) if s else part for s in shifts], axis=0)
            for part in (spread[b * cols : (b + 1) * cols] for b in range(blocks))
        ],
        axis=1,
    )
    scores = SCALE * lax.dot_general(q, k, nt, preferred_element_type=F32) + bias
    scores = jnp.where(allowed, scores, -1e30)
    weights = jnp.exp(scores - jnp.max(scores, axis=1, keepdims=True))
    probs = weights / jnp.sum(weights, axis=1, keepdims=True)
    grad_prob = lax.dot_general(g, v, nt, preferred_element_type=F32)
    grad_prob = jnp.where(allowed, grad_prob, 0.0)
    delta = jnp.sum(probs * grad_prob, axis=1, keepdims=True)
    dscore = probs * (grad_prob - delta)
    folded = []
    for b in range(blocks):
        total = None
        for i, s in enumerate(shifts):
            part = dscore[i * cols : (i + 1) * cols, b * span : (b + 1) * span]
            part = pltpu.roll(part, (span - s) % span, 1) if s else part
            total = part if total is None else total + part
        folded.append(total)
    low = dscore.astype(BF16)
    prob_low = probs.astype(BF16)
    grad_q = SCALE * jnp.dot(low, k, preferred_element_type=F32)
    grad_k = SCALE * lax.dot_general(low, q, tn, preferred_element_type=F32)
    grad_v = lax.dot_general(prob_low, g, tn, preferred_element_type=F32)
    return grad_q, grad_k, grad_v, folded


def mega_kernel(
    dims,
    sizes,
    valid,
    diag,
    q,
    keys,
    values,
    grad_out,
    w_out,
    gq,
    gk,
    gv,
    table,
    features,
    kv,
    feat,
    part,
    back,
    grad_attn,
    gkv,
    gsend,
    gmid,
    grim,
    fold,
    tables,
    feat_out_sem,
    feat_sem,
    pass_sem,
    part_out_sem,
    part_sem,
    kv_out_sem,
    kv_sem,
    g_out_sem,
    g_sem,
    t_out_sem,
    t_sem,
    own_sem,
):
    rows, cols, slots, blocks = dims
    lat_size, lon_size, chan_size = sizes
    tokens, width = q.shape
    heads = width // HEAD_DIM
    span, rim = slots * cols, REACH * cols
    depth = w_out.shape[0]
    slices = grad_out.shape[0]
    group = lat_size * lon_size
    lat, lon, chan = lax.axis_index("lat"), lax.axis_index("lon"), lax.axis_index("chan")
    me = lat * lon_size + lon
    source_chan = me // slices
    mesh_id = pl.DeviceIdType.MESH

    def remote(src, dst, send, recv, where):
        return pltpu.make_async_remote_copy(
            src_ref=src,
            dst_ref=dst,
            send_sem=send,
            recv_sem=recv,
            device_id=where,
            device_id_type=mesh_id,
        )

    def place(index):
        return index // lon_size, lax.rem(index, lon_size)

    total_devices = group * chan_size
    mine = me * chan_size + chan
    barrier = pltpu.get_barrier_semaphore()

    def greet(step, carry):
        other = lax.rem(mine + step, total_devices)
        to_lat, to_lon = place(other // chan_size)
        pl.semaphore_signal(
            barrier,
            inc=1,
            device_id=(to_lat, to_lon, lax.rem(other, chan_size)),
            device_id_type=mesh_id,
        )
        return carry

    lax.fori_loop(1, total_devices, greet, 0)
    own_copies = [
        pltpu.make_async_copy(x, kv.at[i, 0, pl.ds(rim, tokens)], own_sem.at[i])
        for i, x in enumerate((keys, values))
    ]
    for copy in own_copies:
        copy.start()
    pl.semaphore_wait(barrier, total_devices - 1)

    def block_at(index):
        return pl.ds(pl.multiple_of(index * tokens, tokens), tokens)

    def feature_copy(i, j):
        target = chan * slices + i
        to_lat, to_lon = place(target)
        to_chan = 2 * j + lax.rem(chan, 2)
        away = (target != me) | (to_chan != chan)
        src, dst = grad_out.at[i], feat.at[block_at(me)]
        out = remote(
            src, dst, feat_out_sem.at[i, j], feat_sem.at[me], (to_lat, to_lon, to_chan)
        )
        return away, out, pltpu.make_async_copy(src, dst, feat_sem.at[me])

    for i in range(slices):
        for j in range(chan_size // 2):
            away, out, own = feature_copy(i, j)
            pl.when(away)(out.start)
            pl.when(jnp.logical_not(away))(own.start)

    def rim_pieces():
        pieces = []
        for b in range(blocks):
            to_lon = lax.rem(lon + (0, lon_size - 1, 1)[b], lon_size)
            from_lon = lax.rem(lon + (0, 1, lon_size - 1)[b], lon_size)
            for d, (shift, own, ext) in enumerate(
                (
                    (0, (0, tokens), (rim, tokens)),
                    (1, (tokens - rim, rim), (0, rim)),
                    (-1, (0, rim), (rim + tokens, rim)),
                )
            ):
                if b or d:
                    pieces.append((b, d, shift, own, ext, to_lon, from_lon))
        return pieces

    def inside(shift):
        return (lat + shift >= 0) & (lat + shift < lat_size)

    def kv_copy(piece, i):
        b, d, shift, own, ext, to_lon, _ = piece
        return remote(
            (keys, values)[i].at[pl.ds(*own)],
            kv.at[i, b, pl.ds(*ext)],
            kv_out_sem.at[i, b, d],
            kv_sem.at[i, b, d],
            (lat + shift, to_lon, chan),
        )

    for piece in rim_pieces():
        for i in range(2):
            pl.when(inside(piece[2]))(kv_copy(piece, i).start)

    last = 2 * rim + tokens
    for i in range(2):
        for b in range(blocks):
            if span > last:
                kv[i, b, pl.ds(last, span - last), :] = jnp.zeros((span - last, width), BF16)

            @pl.when(lat == 0)
            def _():
                kv[i, b, pl.ds(0, rim), :] = jnp.zeros((rim, width), BF16)

            @pl.when(lat == lat_size - 1)
            def _():
                kv[i, b, pl.ds(rim + tokens, rim), :] = jnp.zeros((rim, width), BF16)

    lat_first = lat * rows
    primary = lax.rem(source_chan, 2) == lax.rem(chan, 2)

    def pass_copy(index):
        sibling = chan + 1 - 2 * lax.rem(chan, 2)
        at = feat.at[block_at(index)]
        return remote(at, at, pass_sem.at[index], feat_sem.at[index], (lat, lon, sibling))

    def part_copy(index):
        to_lat, to_lon = place(index)
        return remote(
            part.at[block_at(index)],
            back.at[block_at(me)],
            part_out_sem.at[index],
            part_sem.at[me],
            (to_lat, to_lon, chan),
        )

    def part_arrival(index):
        at_lat, at_lon = place(index)
        return remote(
            part.at[block_at(index)],
            back.at[block_at(index)],
            part_out_sem.at[index],
            part_sem.at[index],
            (at_lat, at_lon, chan),
        )

    def one_block(step, carry):
        index = lax.rem(me + step, group)
        at = feat.at[block_at(index)]
        is_own = (index == me) & (source_chan == chan)
        local_copy = pltpu.make_async_copy(grad_out.at[0], at, feat_sem.at[index])
        arrival = remote(at, at, pass_sem.at[index], feat_sem.at[index], (lat, lon, chan))
        pl.when(is_own)(local_copy.wait)
        pl.when(jnp.logical_not(is_own))(arrival.wait_recv)
        pl.when(primary)(pass_copy(index).start)
        product = jnp.dot(
            feat[block_at(index), :], w_out[...], preferred_element_type=F32
        ).astype(BF16)

        @pl.when(index == me)
        def _():
            back[block_at(me), :] = product

        @pl.when(index != me)
        def _():
            part[block_at(index), :] = product
            part_copy(index).start()

        return carry

    lax.fori_loop(0, group, one_block, 0)
    features_copy = pltpu.make_async_copy(feat, features, own_sem.at[2])
    features_copy.start()

    allowed = allowed_pairs(
        valid[...], lat_first, lat_size * rows, rows, cols, slots, blocks, lon_size
    )
    spread = expand_bias(diag[...], cols, slots)
    for copy in own_copies:
        copy.wait()
    for piece in rim_pieces():
        for i in range(2):
            pl.when(inside(-piece[2]))(kv_copy(piece, i).wait_recv)

    def add_block(step, total):
        index = lax.rem(me + step, group)
        part_arrival(index).wait_recv()
        return total + back[block_at(index), :].astype(F32)

    own = back[block_at(me), :].astype(F32)
    grad_attn[...] = lax.fori_loop(1, group, add_block, own).astype(BF16)

    for h in range(heads):
        at = pl.ds(h * HEAD_DIM, HEAD_DIM)
        head_bias = spread[h * blocks * cols : (h + 1) * blocks * cols]
        grad_q, grad_k, grad_v, folded = attend(
            dims,
            allowed,
            head_bias,
            q[:, at],
            grad_attn[:, at],
            kv[0, :, :, at].reshape(blocks * span, HEAD_DIM),
            kv[1, :, :, at].reshape(blocks * span, HEAD_DIM),
        )
        gq[:, at] = grad_q.astype(BF16)
        for i, grad in enumerate((grad_k, grad_v)):
            gkv[i, :, at] = grad[rim : rim + tokens]
            gsend[i, :, :, at] = grad.astype(BF16).reshape(blocks, span, HEAD_DIM)
        for b in range(blocks):
            fold[pl.ds((h * blocks + b) * cols, cols), :] = folded[b]

    def grad_copy(piece, i):
        b, d, shift, _, ext, _, from_lon = piece
        dst = gmid.at[i, b] if d == 0 else grim.at[i, b, d - 1]
        return remote(
            gsend.at[i, b, pl.ds(*ext)],
            dst,
            g_out_sem.at[i, b, d],
            g_sem.at[i, b, d],
            (lat - shift, from_lon, chan),
        )

    for piece in rim_pieces():
        for i in range(2):
            pl.when(inside(-piece[2]))(grad_copy(piece, i).start)

    tables[me] = collapse_bias(fold[...], cols, slots)

    def table_copy(index, slot):
        to_lat, to_lon = place(index)
        return remote(
            tables.at[me],
            tables.at[slot],
            t_out_sem.at[index],
            t_sem.at[slot],
            (to_lat, to_lon, chan),
        )

    def start_table(step, carry):
        table_copy(lax.rem(me + step, group), me).start()
        return carry

    lax.fori_loop(1, group, start_table, 0)

    for i in range(2):
        for piece in rim_pieces():
            b, d, shift, own, *_ = piece

            @pl.when(inside(shift))
            def _():
                grad_copy(piece, i).wait_recv()
                part_in = gmid[i, b] if d == 0 else grim[i, b, d - 1]
                gkv[i, pl.ds(*own), :] = gkv[i, pl.ds(*own), :] + part_in.astype(F32)

        (gk, gv)[i][...] = gkv[i].astype(BF16)

    def add_table(step, total):
        index = lax.rem(me + step, group)
        table_copy(index, index).wait_recv()
        return total + tables[index]

    table[...] = lax.fori_loop(1, group, add_table, tables[me])

    for i in range(slices):
        for j in range(chan_size // 2):
            away, out, _ = feature_copy(i, j)
            pl.when(away)(out.wait_send)
    for piece in rim_pieces():
        for i in range(2):
            pl.when(inside(piece[2]))(kv_copy(piece, i).wait_send)
            pl.when(inside(-piece[2]))(grad_copy(piece, i).wait_send)

    def sent(step, carry):
        index = lax.rem(me + step, group)
        pl.when(primary)(pass_copy(index).wait_send)

        @pl.when(step > 0)
        def _():
            part_copy(index).wait_send()
            table_copy(index, me).wait_send()

        return carry

    lax.fori_loop(0, group, sent, 0)
    features_copy.wait()


def diag_table(table, cols, slots, blocks, lon_size):
    heads, height, width = table.shape

    def placed(part, first):
        return jnp.pad(part, ((0, 0), (0, 0), (first, 2 * cols - first - part.shape[2])))

    own = placed(table, cols - 1 - REACH)
    right = placed(table[:, :, REACH + 1 :], 0) if blocks > 1 else None
    left = placed(table[:, :, :REACH], 2 * cols - 1 - REACH) if blocks > 1 else None
    parts = [own] if blocks == 1 else [own, right + left] if lon_size == 2 else [own, right, left]
    stacked = jnp.stack(parts, axis=1)
    stacked = jnp.pad(stacked, ((0, 0), (0, 0), (0, slots - height), (0, 0)))
    return stacked.reshape(heads * blocks, slots * 2 * cols)


def undiag_table(diag, heads, cols, slots, blocks, lon_size):
    grid = diag.reshape(heads, blocks, slots, 2 * cols)[:, :, : 2 * WIN - 1]
    first = cols - 1 - REACH
    own = grid[:, 0, :, first : first + WIN]
    if blocks == 1:
        return own
    right = grid[:, 1, :, :REACH]
    left = grid[:, blocks - 1, :, 2 * cols - 1 - REACH : 2 * cols - 1]
    gap = jnp.zeros(own.shape[:2] + (1,), own.dtype)
    return own + jnp.concatenate([left, gap, right], axis=2)


def valid_row(key_mask, rows, cols, slots, blocks, lon_size):
    lat_total, lon_total = key_mask.shape
    mark = (jnp.arange(lat_total) % 4 == 0)[:, None] & (jnp.arange(lon_total) % 4 == 0)[None, :]
    valid = ((key_mask == 1) | mark).astype(jnp.int32)
    valid = jnp.pad(valid, ((REACH, slots), (0, 0)))
    valid = lax.dynamic_slice_in_dim(valid, lax.axis_index("lat") * rows, slots, 0)
    me = lax.axis_index("lon")
    parts = [
        lax.dynamic_slice_in_dim(valid, (me + step) % lon_size * cols, cols, 1)
        for step in (0, 1, lon_size - 1)[:blocks]
    ]
    return jnp.stack(parts, axis=0).reshape(1, blocks * slots * cols)


def local(queries, keys, values, attn_out, grad_out, w_out, bias_table, key_mask):
    rows, cols, width = queries.shape
    heads = bias_table.shape[0]
    tokens = rows * cols
    lat_size, lon_size = lax.axis_size("lat"), lax.axis_size("lon")
    blocks = min(3, lon_size)
    slots = row_slots(rows, cols)
    span = slots * cols
    rim = REACH * cols
    group = ("lat", "lon")
    dims = (rows, cols, slots, blocks)
    depth = w_out.shape[0]
    sizes = (lat_size, lon_size, lax.axis_size("chan"))
    count = lat_size * lon_size
    saved = lax.all_gather(attn_out.reshape(tokens, width), group, axis=0, tiled=True)
    slices = grad_out.reshape(tokens, -1, depth).transpose(1, 0, 2)
    diag = diag_table(bias_table, cols, slots, blocks, lon_size)
    valid = valid_row(key_mask, rows, cols, slots, blocks, lon_size)
    vmem = pl.BlockSpec(memory_space=pltpu.VMEM)
    anywhere = pl.BlockSpec(memory_space=pl.ANY)
    dma = pltpu.SemaphoreType.DMA
    token = jax.ShapeDtypeStruct((tokens, width), BF16)
    table_shape = (heads * blocks, slots * 2 * cols)
    grad_queries, grad_keys, grad_values, diag_grad, features = pl.pallas_call(
        functools.partial(mega_kernel, dims, sizes),
        out_shape=(
            token,
            token,
            token,
            jax.ShapeDtypeStruct(table_shape, F32),
            jax.ShapeDtypeStruct((count * tokens, depth), BF16),
        ),
        in_specs=[vmem] * 7,
        out_specs=(vmem, vmem, vmem, vmem, anywhere),
        scratch_shapes=[
            pltpu.VMEM((2, blocks, span, width), BF16),
            pltpu.VMEM((count * tokens, depth), BF16),
            pltpu.VMEM((count * tokens, width), BF16),
            pltpu.VMEM((count * tokens, width), BF16),
            pltpu.VMEM((tokens, width), BF16),
            pltpu.VMEM((2, tokens, width), F32),
            pltpu.VMEM((2, blocks, span, width), BF16),
            pltpu.VMEM((2, blocks, tokens, width), BF16),
            pltpu.VMEM((2, blocks, 2, rim, width), BF16),
            pltpu.VMEM((heads * blocks * cols, span), F32),
            pltpu.VMEM((count,) + table_shape, F32),
            dma((slices.shape[0], sizes[2] // 2)),
            dma((count,)),
            dma((count,)),
            dma((count,)),
            dma((count,)),
            dma((2, blocks, 3)),
            dma((2, blocks, 3)),
            dma((2, blocks, 3)),
            dma((2, blocks, 3)),
            dma((count,)),
            dma((count,)),
            dma((3,)),
        ],
        compiler_params=pltpu.CompilerParams(
            collective_id=0, has_side_effects=True, vmem_limit_bytes=56 * 1024 * 1024
        ),
    )(
        valid,
        diag,
        queries.reshape(tokens, width),
        keys.reshape(tokens, width),
        values.reshape(tokens, width),
        slices,
        w_out,
    )
    grad_table = undiag_table(diag_grad, heads, cols, slots, blocks, lon_size)
    grad_wout = lax.dot_general(
        features, saved, (((0,), (0,)), ((), ())), preferred_element_type=F32
    )
    tokens_out = [x.reshape(rows, cols, width) for x in (grad_queries, grad_keys, grad_values)]
    return (*tokens_out, grad_wout, grad_table)


def solution(mesh):
    token = P("lat", "lon", "chan")
    matrix = P(("lat", "lon"), "chan")
    table = P("chan", None, None)
    return jax.shard_map(
        local,
        mesh=mesh,
        in_specs=(token, token, token, token, token, matrix, table, P()),
        out_specs=(token, token, token, matrix, table),
        check_vma=False,
    )
```

```python
import functools

import jax
import jax.numpy as jnp
from jax import lax
from jax.experimental import pallas as pl
from jax.experimental.pallas import tpu as pltpu
from jax.sharding import PartitionSpec as P

HEAD_DIM = 128
WIN = 13
REACH = WIN // 2
SCALE = HEAD_DIM ** (-0.5)
F32 = jnp.float32
BF16 = jnp.bfloat16


def row_slots(rows, cols):
    slots = max(rows + 2 * REACH, 2 * WIN - 1)
    while slots * cols % 128:
        slots += 1
    return slots


def column_pick(cols, slots):
    wide, tight = slots * 2 * cols, slots * cols
    source = lax.broadcasted_iota(jnp.int32, (wide, tight), 0)
    lane = lax.broadcasted_iota(jnp.int32, (wide, tight), 1)
    return (source == lane // cols * (2 * cols) + lane % cols).astype(F32)


def skew(value, cols, left):
    lanes = value.shape[1]
    place = lax.broadcasted_iota(jnp.int32, value.shape, 0) % cols
    step = 1
    while step < cols:
        moved = pltpu.roll(value, lanes - step if left else step, 1)
        value = jnp.where(place // step % 2 == 1, moved, value)
        step *= 2
    return value


def expand_bias(diag, cols, slots):
    lanes = diag.shape[1]
    rows = [jnp.broadcast_to(diag[i : i + 1], (cols, lanes)) for i in range(diag.shape[0])]
    wide = pltpu.roll(jnp.concatenate(rows, axis=0), lanes - (cols - 1), 1)
    wide = skew(wide, cols, False)
    return jnp.dot(
        wide, column_pick(cols, slots), precision=lax.Precision.HIGHEST, preferred_element_type=F32
    )


def collapse_bias(spread, cols, slots):
    wide = lax.dot_general(
        spread,
        column_pick(cols, slots),
        (((1,), (1,)), ((), ())),
        precision=lax.Precision.HIGHEST,
        preferred_element_type=F32,
    )
    wide = skew(pltpu.roll(wide, cols - 1, 1), cols, True)
    return jnp.sum(wide.reshape(-1, cols, wide.shape[1]), axis=1)


def allowed_pairs(valid, lat_first, lat_total, rows, cols, slots, blocks, lon_size):
    shape = (rows * cols, blocks * slots * cols)
    query = lax.broadcasted_iota(jnp.int32, shape, 0)
    lane = lax.broadcasted_iota(jnp.int32, shape, 1)
    block = lane // (slots * cols)
    key = lane % (slots * cols)
    row = lat_first + query // cols
    first = jnp.clip(row - REACH, 0, lat_total - WIN)
    key_row = lat_first - REACH + key // cols
    delta = key % cols - query % cols
    in_lat = (key_row >= first) & (key_row < first + WIN)
    near = (delta >= -REACH) & (delta <= REACH)
    right = delta + cols <= REACH
    left = delta - cols >= -REACH
    if blocks == 1:
        in_lon = near
    elif lon_size == 2:
        in_lon = ((block == 0) & near) | ((block == 1) & (right | left))
    else:
        in_lon = ((block == 0) & near) | ((block == 1) & right) | ((block == 2) & left)
    return in_lat & in_lon & (valid > 0)


def attend(dims, allowed, spread, q, g, k, v):
    rows, cols, slots, blocks = dims
    span = slots * cols
    nt = (((1,), (1,)), ((), ()))
    tn = (((0,), (0,)), ((), ()))
    shifts = [((i - REACH) * cols) % span for i in range(rows)]
    bias = jnp.concatenate(
        [
            jnp.concatenate([pltpu.roll(part, s, 1) if s else part for s in shifts], axis=0)
            for part in (spread[b * cols : (b + 1) * cols] for b in range(blocks))
        ],
        axis=1,
    )
    scores = SCALE * lax.dot_general(q, k, nt, preferred_element_type=F32) + bias
    scores = jnp.where(allowed, scores, -1e30)
    weights = jnp.exp(scores - jnp.max(scores, axis=1, keepdims=True))
    probs = weights / jnp.sum(weights, axis=1, keepdims=True)
    grad_prob = lax.dot_general(g, v, nt, preferred_element_type=F32)
    grad_prob = jnp.where(allowed, grad_prob, 0.0)
    delta = jnp.sum(probs * grad_prob, axis=1, keepdims=True)
    dscore = probs * (grad_prob - delta)
    folded = []
    for b in range(blocks):
        total = None
        for i, s in enumerate(shifts):
            part = dscore[i * cols : (i + 1) * cols, b * span : (b + 1) * span]
            part = pltpu.roll(part, (span - s) % span, 1) if s else part
            total = part if total is None else total + part
        folded.append(total)
    low = dscore.astype(BF16)
    prob_low = probs.astype(BF16)
    grad_q = SCALE * jnp.dot(low, k, preferred_element_type=F32)
    grad_k = SCALE * lax.dot_general(low, q, tn, preferred_element_type=F32)
    grad_v = lax.dot_general(prob_low, g, tn, preferred_element_type=F32)
    return grad_q, grad_k, grad_v, folded


def mega_kernel(
    dims,
    sizes,
    valid,
    diag,
    q,
    keys,
    values,
    attn,
    grad_out,
    w_out,
    gq,
    gk,
    gv,
    table,
    wout,
    kv,
    feat,
    part,
    side,
    ready,
    own_part,
    back,
    saved,
    grad_attn,
    gkv,
    gsend,
    gmid,
    grim,
    fold,
    tables,
    feat_out_sem,
    feat_sem,
    pass_sem,
    part_out_sem,
    side_sem,
    back_out_sem,
    back_sem,
    saved_out_sem,
    saved_on_sem,
    saved_sem,
    kv_out_sem,
    kv_sem,
    g_out_sem,
    g_sem,
    t_out_sem,
    t_sem,
    own_sem,
):
    rows, cols, slots, blocks = dims
    lat_size, lon_size, chan_size = sizes
    tokens, width = q.shape
    heads = width // HEAD_DIM
    span, rim = slots * cols, REACH * cols
    depth = w_out.shape[0]
    slices = grad_out.shape[0]
    group = lat_size * lon_size
    lat, lon, chan = lax.axis_index("lat"), lax.axis_index("lon"), lax.axis_index("chan")
    me = lat * lon_size + lon
    source_chan = me // slices
    mesh_id = pl.DeviceIdType.MESH

    def remote(src, dst, send, recv, where):
        return pltpu.make_async_remote_copy(
            src_ref=src,
            dst_ref=dst,
            send_sem=send,
            recv_sem=recv,
            device_id=where,
            device_id_type=mesh_id,
        )

    def place(index):
        return index // lon_size, lax.rem(index, lon_size)

    total_devices = group * chan_size
    mine = me * chan_size + chan
    barrier = pltpu.get_barrier_semaphore()

    def greet(step, carry):
        other = lax.rem(mine + step, total_devices)
        to_lat, to_lon = place(other // chan_size)
        pl.semaphore_signal(
            barrier,
            inc=1,
            device_id=(to_lat, to_lon, lax.rem(other, chan_size)),
            device_id_type=mesh_id,
        )
        return carry

    lax.fori_loop(1, total_devices, greet, 0)
    own_copies = [
        pltpu.make_async_copy(x, kv.at[i, 0, pl.ds(rim, tokens)], own_sem.at[i])
        for i, x in enumerate((keys, values))
    ]
    own_at = pl.ds(pl.multiple_of(me * tokens, tokens), tokens)
    own_copies.append(pltpu.make_async_copy(attn, saved.at[own_at], own_sem.at[2]))
    for copy in own_copies:
        copy.start()
    pl.semaphore_wait(barrier, total_devices - 1)

    def block_at(index):
        return pl.ds(pl.multiple_of(index * tokens, tokens), tokens)

    def feature_copy(i, j):
        target = chan * slices + i
        to_lat, to_lon = place(target)
        to_chan = 2 * j + lax.rem(chan, 2)
        away = (target != me) | (to_chan != chan)
        src, dst = grad_out.at[i], feat.at[block_at(me)]
        out = remote(
            src, dst, feat_out_sem.at[i, j], feat_sem.at[me], (to_lat, to_lon, to_chan)
        )
        return away, out, (src, dst, feat_sem.at[me])

    for i in range(slices):
        for j in range(chan_size // 2):
            away, out, own = feature_copy(i, j)
            pl.when(away)(out.start)
            pl.when(jnp.logical_not(away))(lambda own=own: pltpu.make_async_copy(*own).start())

    def rim_pieces():
        pieces = []
        for b in range(blocks):
            to_lon = lax.rem(lon + (0, lon_size - 1, 1)[b], lon_size)
            from_lon = lax.rem(lon + (0, 1, lon_size - 1)[b], lon_size)
            for d, (shift, own, ext) in enumerate(
                (
                    (0, (0, tokens), (rim, tokens)),
                    (1, (tokens - rim, rim), (0, rim)),
                    (-1, (0, rim), (rim + tokens, rim)),
                )
            ):
                if b or d:
                    pieces.append((b, d, shift, own, ext, to_lon, from_lon))
        return pieces

    def inside(shift):
        return (lat + shift >= 0) & (lat + shift < lat_size)

    def kv_copy(piece, i):
        b, d, shift, own, ext, to_lon, _ = piece
        return remote(
            (keys, values)[i].at[pl.ds(*own)],
            kv.at[i, b, pl.ds(*ext)],
            kv_out_sem.at[i, b, d],
            kv_sem.at[i, b, d],
            (lat + shift, to_lon, chan),
        )

    for piece in rim_pieces():
        for i in range(2):
            pl.when(inside(piece[2]))(kv_copy(piece, i).start)

    last = 2 * rim + tokens
    for i in range(2):
        for b in range(blocks):
            if span > last:
                kv[i, b, pl.ds(last, span - last), :] = jnp.zeros((span - last, width), BF16)

            @pl.when(lat == 0)
            def _():
                kv[i, b, pl.ds(0, rim), :] = jnp.zeros((rim, width), BF16)

            @pl.when(lat == lat_size - 1)
            def _():
                kv[i, b, pl.ds(rim + tokens, rim), :] = jnp.zeros((rim, width), BF16)

    lat_first = lat * rows
    primary = lax.rem(source_chan, 2) == lax.rem(chan, 2)

    def pass_copy(index):
        sibling = chan + 1 - 2 * lax.rem(chan, 2)
        at = feat.at[block_at(index)]
        return remote(at, at, pass_sem.at[index], feat_sem.at[index], (lat, lon, sibling))

    def part_copy(index):
        to_lat, to_lon = place(index)
        return remote(
            part.at[block_at(index)],
            side.at[lon, to_lat],
            part_out_sem.at[index],
            side_sem.at[lon, to_lat],
            (lat, to_lon, chan),
        )

    def side_arrival(from_lon, row_block):
        return remote(
            side.at[from_lon, row_block],
            side.at[from_lon, row_block],
            part_out_sem.at[0],
            side_sem.at[from_lon, row_block],
            (lat, from_lon, chan),
        )

    def back_copy(row_block, slot):
        return remote(
            ready.at[row_block],
            back.at[slot],
            back_out_sem.at[row_block],
            back_sem.at[slot],
            (row_block, lon, chan),
        )

    def saved_copy(to_lat, slot):
        return remote(
            attn,
            saved.at[block_at(slot)],
            saved_out_sem.at[to_lat],
            saved_sem.at[slot],
            (to_lat, lon, chan),
        )

    def saved_pass(row_block, to_lon):
        index = row_block * lon_size + lon
        src = saved.at[block_at(index)]
        return remote(
            src, src, saved_on_sem.at[row_block, to_lon], saved_sem.at[index], (lat, to_lon, chan)
        )

    def saved_arrival(index):
        at = saved.at[block_at(index)]
        return remote(at, at, saved_out_sem.at[0], saved_sem.at[index], (lat, lon, chan))

    def one_block(step, carry):
        at_lat = lax.rem(lat + 1 + step // lon_size, lat_size)
        at_lon = lax.rem(lon + 1 + lax.rem(step, lon_size), lon_size)
        index = at_lat * lon_size + at_lon
        at = feat.at[block_at(index)]
        is_own = (index == me) & (source_chan == chan)
        local_copy = pltpu.make_async_copy(grad_out.at[0], at, feat_sem.at[index])
        arrival = remote(at, at, pass_sem.at[index], feat_sem.at[index], (lat, lon, chan))
        pl.when(is_own)(local_copy.wait)
        pl.when(jnp.logical_not(is_own))(arrival.wait_recv)
        pl.when(primary)(pass_copy(index).start)
        product = jnp.dot(
            feat[block_at(index), :], w_out[...], preferred_element_type=F32
        )

        part[block_at(index), :] = product.astype(BF16)

        @pl.when(at_lon == lon)
        def _():
            own_part[at_lat] = product

        @pl.when(at_lon != lon)
        def _():
            part_copy(index).start()

        return carry

    lax.fori_loop(0, group, one_block, 0)

    def one_sum(step, carry):
        row_block = lax.rem(lat + step, lat_size)

        def add_side(turn, total):
            from_lon = lax.rem(lon + turn, lon_size)
            side_arrival(from_lon, row_block).wait_recv()
            return total + side[from_lon, row_block].astype(F32)

        total = lax.fori_loop(1, lon_size, add_side, own_part[row_block])
        own_part[row_block] = total

        @pl.when(row_block != lat)
        def _():
            ready[row_block] = total.astype(BF16)
            back_copy(row_block, lat).start()

        return carry

    lax.fori_loop(1, lat_size + 1, one_sum, 0)

    def start_saved(step, carry):
        saved_copy(lax.rem(lat + step, lat_size), me).start()
        return carry

    lax.fori_loop(1, lat_size, start_saved, 0)

    allowed = allowed_pairs(
        valid[...], lat_first, lat_size * rows, rows, cols, slots, blocks, lon_size
    )
    spread = expand_bias(diag[...], cols, slots)
    for copy in own_copies:
        copy.wait()
    for piece in rim_pieces():
        for i in range(2):
            pl.when(inside(-piece[2]))(kv_copy(piece, i).wait_recv)

    def add_block(step, total):
        row_block = lax.rem(lat + step, lat_size)
        back_copy(row_block, row_block).wait_recv()
        return total + back[row_block].astype(F32)

    grad_attn[...] = lax.fori_loop(1, lat_size, add_block, own_part[lat]).astype(BF16)

    for h in range(heads):
        at = pl.ds(h * HEAD_DIM, HEAD_DIM)
        head_bias = spread[h * blocks * cols : (h + 1) * blocks * cols]
        grad_q, grad_k, grad_v, folded = attend(
            dims,
            allowed,
            head_bias,
            q[:, at],
            grad_attn[:, at],
            kv[0, :, :, at].reshape(blocks * span, HEAD_DIM),
            kv[1, :, :, at].reshape(blocks * span, HEAD_DIM),
        )
        gq[:, at] = grad_q.astype(BF16)
        for i, grad in enumerate((grad_k, grad_v)):
            gkv[i, :, at] = grad[rim : rim + tokens]
            gsend[i, :, :, at] = grad.astype(BF16).reshape(blocks, span, HEAD_DIM)
        for b in range(blocks):
            fold[pl.ds((h * blocks + b) * cols, cols), :] = folded[b]

    def grad_copy(piece, i):
        b, d, shift, _, ext, _, from_lon = piece
        dst = gmid.at[i, b] if d == 0 else grim.at[i, b, d - 1]
        return remote(
            gsend.at[i, b, pl.ds(*ext)],
            dst,
            g_out_sem.at[i, b, d],
            g_sem.at[i, b, d],
            (lat - shift, from_lon, chan),
        )

    for piece in rim_pieces():
        for i in range(2):
            pl.when(inside(-piece[2]))(grad_copy(piece, i).start)

    tables[me] = collapse_bias(fold[...], cols, slots)

    def table_copy(index, slot):
        to_lat, to_lon = place(index)
        return remote(
            tables.at[me],
            tables.at[slot],
            t_out_sem.at[index],
            t_sem.at[slot],
            (to_lat, to_lon, chan),
        )

    def start_table(step, carry):
        table_copy(lax.rem(me + step, group), me).start()
        return carry

    lax.fori_loop(1, group, start_table, 0)

    def pass_saved(step, carry):
        row_block = lax.rem(lat + step, lat_size)

        @pl.when(step > 0)
        def _():
            saved_arrival(row_block * lon_size + lon).wait_recv()

        def to_side(turn, carry):
            saved_pass(row_block, lax.rem(lon + turn, lon_size)).start()
            return carry

        return lax.fori_loop(1, lon_size, to_side, carry)

    lax.fori_loop(0, lat_size, pass_saved, 0)

    for i in range(2):
        for piece in rim_pieces():
            b, d, shift, own, *_ = piece

            @pl.when(inside(shift))
            def _():
                grad_copy(piece, i).wait_recv()
                part_in = gmid[i, b] if d == 0 else grim[i, b, d - 1]
                gkv[i, pl.ds(*own), :] = gkv[i, pl.ds(*own), :] + part_in.astype(F32)

        (gk, gv)[i][...] = gkv[i].astype(BF16)

    def add_table(step, total):
        index = lax.rem(me + step, group)
        table_copy(index, index).wait_recv()
        return total + tables[index]

    table[...] = lax.fori_loop(1, group, add_table, tables[me])

    def await_saved(step, carry):
        row_block, turn = step // (lon_size - 1), lax.rem(step, lon_size - 1)
        from_lon = lax.rem(lon + 1 + turn, lon_size)
        saved_arrival(row_block * lon_size + from_lon).wait_recv()
        return carry

    if lon_size > 1:
        lax.fori_loop(0, lat_size * (lon_size - 1), await_saved, 0)
    strip = 128 if width % 128 == 0 else width
    for start in range(0, width, strip):
        wout[:, pl.ds(start, strip)] = lax.dot_general(
            feat[...],
            saved[:, pl.ds(start, strip)],
            (((0,), (0,)), ((), ())),
            preferred_element_type=F32,
        )

    for i in range(slices):
        for j in range(chan_size // 2):
            away, out, _ = feature_copy(i, j)
            pl.when(away)(out.wait_send)
    for piece in rim_pieces():
        for i in range(2):
            pl.when(inside(piece[2]))(kv_copy(piece, i).wait_send)
            pl.when(inside(-piece[2]))(grad_copy(piece, i).wait_send)

    def sent(step, carry):
        index = lax.rem(me + step, group)
        pl.when(primary)(pass_copy(index).wait_send)

        _, at_lon = place(index)

        @pl.when(at_lon != lon)
        def _():
            part_copy(index).wait_send()
            saved_pass(index // lon_size, at_lon).wait_send()

        @pl.when(step > 0)
        def _():
            table_copy(index, me).wait_send()

        return carry

    lax.fori_loop(0, group, sent, 0)

    def sent_rows(step, carry):
        row_block = lax.rem(lat + step, lat_size)
        back_copy(row_block, lat).wait_send()
        saved_copy(row_block, me).wait_send()
        return carry

    lax.fori_loop(1, lat_size, sent_rows, 0)


def diag_table(table, cols, slots, blocks, lon_size):
    heads, height, width = table.shape

    def placed(part, first):
        return jnp.pad(part, ((0, 0), (0, 0), (first, 2 * cols - first - part.shape[2])))

    own = placed(table, cols - 1 - REACH)
    right = placed(table[:, :, REACH + 1 :], 0) if blocks > 1 else None
    left = placed(table[:, :, :REACH], 2 * cols - 1 - REACH) if blocks > 1 else None
    parts = [own] if blocks == 1 else [own, right + left] if lon_size == 2 else [own, right, left]
    stacked = jnp.stack(parts, axis=1)
    stacked = jnp.pad(stacked, ((0, 0), (0, 0), (0, slots - height), (0, 0)))
    return stacked.reshape(heads * blocks, slots * 2 * cols)


def undiag_table(diag, heads, cols, slots, blocks, lon_size):
    grid = diag.reshape(heads, blocks, slots, 2 * cols)[:, :, : 2 * WIN - 1]
    first = cols - 1 - REACH
    own = grid[:, 0, :, first : first + WIN]
    if blocks == 1:
        return own
    right = grid[:, 1, :, :REACH]
    left = grid[:, blocks - 1, :, 2 * cols - 1 - REACH : 2 * cols - 1]
    gap = jnp.zeros(own.shape[:2] + (1,), own.dtype)
    return own + jnp.concatenate([left, gap, right], axis=2)


def valid_row(key_mask, rows, cols, slots, blocks, lon_size):
    lat_total, lon_total = key_mask.shape
    mark = (jnp.arange(lat_total) % 4 == 0)[:, None] & (jnp.arange(lon_total) % 4 == 0)[None, :]
    valid = ((key_mask == 1) | mark).astype(jnp.int32)
    valid = jnp.pad(valid, ((REACH, slots), (0, 0)))
    valid = lax.dynamic_slice_in_dim(valid, lax.axis_index("lat") * rows, slots, 0)
    me = lax.axis_index("lon")
    parts = [
        lax.dynamic_slice_in_dim(valid, (me + step) % lon_size * cols, cols, 1)
        for step in (0, 1, lon_size - 1)[:blocks]
    ]
    return jnp.stack(parts, axis=0).reshape(1, blocks * slots * cols)


def local(queries, keys, values, attn_out, grad_out, w_out, bias_table, key_mask):
    rows, cols, width = queries.shape
    heads = bias_table.shape[0]
    tokens = rows * cols
    lat_size, lon_size = lax.axis_size("lat"), lax.axis_size("lon")
    blocks = min(3, lon_size)
    slots = row_slots(rows, cols)
    span = slots * cols
    rim = REACH * cols
    group = ("lat", "lon")
    dims = (rows, cols, slots, blocks)
    depth = w_out.shape[0]
    sizes = (lat_size, lon_size, lax.axis_size("chan"))
    count = lat_size * lon_size
    slices = grad_out.reshape(tokens, -1, depth).transpose(1, 0, 2)
    diag = diag_table(bias_table, cols, slots, blocks, lon_size)
    valid = valid_row(key_mask, rows, cols, slots, blocks, lon_size)
    vmem = pl.BlockSpec(memory_space=pltpu.VMEM)
    dma = pltpu.SemaphoreType.DMA
    token = jax.ShapeDtypeStruct((tokens, width), BF16)
    table_shape = (heads * blocks, slots * 2 * cols)
    grad_queries, grad_keys, grad_values, diag_grad, grad_wout = pl.pallas_call(
        functools.partial(mega_kernel, dims, sizes),
        out_shape=(
            token,
            token,
            token,
            jax.ShapeDtypeStruct(table_shape, F32),
            jax.ShapeDtypeStruct((depth, width), F32),
        ),
        in_specs=[vmem] * 8,
        out_specs=(vmem,) * 5,
        scratch_shapes=[
            pltpu.VMEM((2, blocks, span, width), BF16),
            pltpu.VMEM((count * tokens, depth), BF16),
            pltpu.VMEM((count * tokens, width), BF16),
            pltpu.VMEM((lon_size, lat_size, tokens, width), BF16),
            pltpu.VMEM((lat_size, tokens, width), BF16),
            pltpu.VMEM((lat_size, tokens, width), F32),
            pltpu.VMEM((lat_size, tokens, width), BF16),
            pltpu.VMEM((count * tokens, width), BF16),
            pltpu.VMEM((tokens, width), BF16),
            pltpu.VMEM((2, tokens, width), F32),
            pltpu.VMEM((2, blocks, span, width), BF16),
            pltpu.VMEM((2, blocks, tokens, width), BF16),
            pltpu.VMEM((2, blocks, 2, rim, width), BF16),
            pltpu.VMEM((heads * blocks * cols, span), F32),
            pltpu.VMEM((count,) + table_shape, F32),
            dma((slices.shape[0], sizes[2] // 2)),
            dma((count,)),
            dma((count,)),
            dma((count,)),
            dma((lon_size, lat_size)),
            dma((lat_size,)),
            dma((lat_size,)),
            dma((lat_size,)),
            dma((lat_size, lon_size)),
            dma((count,)),
            dma((2, blocks, 3)),
            dma((2, blocks, 3)),
            dma((2, blocks, 3)),
            dma((2, blocks, 3)),
            dma((count,)),
            dma((count,)),
            dma((3,)),
        ],
        compiler_params=pltpu.CompilerParams(
            collective_id=0, has_side_effects=True, vmem_limit_bytes=56 * 1024 * 1024
        ),
    )(
        valid,
        diag,
        queries.reshape(tokens, width),
        keys.reshape(tokens, width),
        values.reshape(tokens, width),
        attn_out.reshape(tokens, width),
        slices,
        w_out,
    )
    grad_table = undiag_table(diag_grad, heads, cols, slots, blocks, lon_size)
    tokens_out = [x.reshape(rows, cols, width) for x in (grad_queries, grad_keys, grad_values)]
    return (*tokens_out, grad_wout, grad_table)


def solution(mesh):
    token = P("lat", "lon", "chan")
    matrix = P(("lat", "lon"), "chan")
    table = P("chan", None, None)
    return jax.shard_map(
        local,
        mesh=mesh,
        in_specs=(token, token, token, token, token, matrix, table, P()),
        out_specs=(token, token, token, matrix, table),
        check_vma=False,
    )
```

```python
import functools

import jax
import jax.numpy as jnp
from jax import lax
from jax.experimental import pallas as pl
from jax.experimental.pallas import tpu as pltpu
from jax.sharding import PartitionSpec as P

HEAD_DIM = 128
WIN = 13
REACH = WIN // 2
SCALE = HEAD_DIM ** (-0.5)
F32 = jnp.float32
BF16 = jnp.bfloat16


def row_slots(rows, cols):
    slots = max(rows + 2 * REACH, 2 * WIN - 1)
    while slots * cols % 128:
        slots += 1
    return slots


def column_pick(cols, slots):
    wide, tight = slots * 2 * cols, slots * cols
    source = lax.broadcasted_iota(jnp.int32, (wide, tight), 0)
    lane = lax.broadcasted_iota(jnp.int32, (wide, tight), 1)
    return (source == lane // cols * (2 * cols) + lane % cols).astype(F32)


def skew(value, cols, left):
    lanes = value.shape[1]
    place = lax.broadcasted_iota(jnp.int32, value.shape, 0) % cols
    step = 1
    while step < cols:
        moved = pltpu.roll(value, lanes - step if left else step, 1)
        value = jnp.where(place // step % 2 == 1, moved, value)
        step *= 2
    return value


def expand_bias(diag, cols, slots):
    lanes = diag.shape[1]
    rows = [jnp.broadcast_to(diag[i : i + 1], (cols, lanes)) for i in range(diag.shape[0])]
    wide = pltpu.roll(jnp.concatenate(rows, axis=0), lanes - (cols - 1), 1)
    wide = skew(wide, cols, False)
    return jnp.dot(
        wide, column_pick(cols, slots), precision=lax.Precision.HIGHEST, preferred_element_type=F32
    )


def collapse_bias(spread, cols, slots):
    wide = lax.dot_general(
        spread,
        column_pick(cols, slots),
        (((1,), (1,)), ((), ())),
        precision=lax.Precision.HIGHEST,
        preferred_element_type=F32,
    )
    wide = skew(pltpu.roll(wide, cols - 1, 1), cols, True)
    return jnp.sum(wide.reshape(-1, cols, wide.shape[1]), axis=1)


def allowed_pairs(valid, lat_first, lat_total, rows, cols, slots, blocks, lon_size):
    shape = (rows * cols, blocks * slots * cols)
    query = lax.broadcasted_iota(jnp.int32, shape, 0)
    lane = lax.broadcasted_iota(jnp.int32, shape, 1)
    block = lane // (slots * cols)
    key = lane % (slots * cols)
    row = lat_first + query // cols
    first = jnp.clip(row - REACH, 0, lat_total - WIN)
    key_row = lat_first - REACH + key // cols
    delta = key % cols - query % cols
    in_lat = (key_row >= first) & (key_row < first + WIN)
    near = (delta >= -REACH) & (delta <= REACH)
    right = delta + cols <= REACH
    left = delta - cols >= -REACH
    if blocks == 1:
        in_lon = near
    elif lon_size == 2:
        in_lon = ((block == 0) & near) | ((block == 1) & (right | left))
    else:
        in_lon = ((block == 0) & near) | ((block == 1) & right) | ((block == 2) & left)
    return in_lat & in_lon & (valid > 0)


def attend(dims, allowed, spread, q, g, k, v):
    rows, cols, slots, blocks = dims
    span = slots * cols
    nt = (((1,), (1,)), ((), ()))
    tn = (((0,), (0,)), ((), ()))
    shifts = [((i - REACH) * cols) % span for i in range(rows)]
    bias = jnp.concatenate(
        [
            jnp.concatenate([pltpu.roll(part, s, 1) if s else part for s in shifts], axis=0)
            for part in (spread[b * cols : (b + 1) * cols] for b in range(blocks))
        ],
        axis=1,
    )
    scores = SCALE * lax.dot_general(q, k, nt, preferred_element_type=F32) + bias
    scores = jnp.where(allowed, scores, -1e30)
    weights = jnp.exp(scores - jnp.max(scores, axis=1, keepdims=True))
    probs = weights / jnp.sum(weights, axis=1, keepdims=True)
    grad_prob = lax.dot_general(g, v, nt, preferred_element_type=F32)
    grad_prob = jnp.where(allowed, grad_prob, 0.0)
    delta = jnp.sum(probs * grad_prob, axis=1, keepdims=True)
    dscore = probs * (grad_prob - delta)
    folded = []
    for b in range(blocks):
        total = None
        for i, s in enumerate(shifts):
            part = dscore[i * cols : (i + 1) * cols, b * span : (b + 1) * span]
            part = pltpu.roll(part, (span - s) % span, 1) if s else part
            total = part if total is None else total + part
        folded.append(total)
    low = dscore.astype(BF16)
    prob_low = probs.astype(BF16)
    grad_q = SCALE * jnp.dot(low, k, preferred_element_type=F32)
    grad_k = SCALE * lax.dot_general(low, q, tn, preferred_element_type=F32)
    grad_v = lax.dot_general(prob_low, g, tn, preferred_element_type=F32)
    return grad_q, grad_k, grad_v, folded


def mega_kernel(
    dims,
    sizes,
    valid,
    diag,
    q,
    keys,
    values,
    attn,
    grad_out,
    w_out,
    gq,
    gk,
    gv,
    table,
    wout,
    kv,
    feat,
    part,
    side,
    ready,
    own_part,
    back,
    saved,
    grad_attn,
    gkv,
    gsend,
    gmid,
    grim,
    fold,
    tables,
    feat_out_sem,
    feat_sem,
    pass_sem,
    relay_sem,
    part_out_sem,
    side_sem,
    back_out_sem,
    back_sem,
    saved_out_sem,
    saved_on_sem,
    saved_sem,
    kv_out_sem,
    kv_sem,
    g_out_sem,
    g_sem,
    t_out_sem,
    t_sem,
    own_sem,
):
    rows, cols, slots, blocks = dims
    lat_size, lon_size, chan_size = sizes
    tokens, width = q.shape
    heads = width // HEAD_DIM
    span, rim = slots * cols, REACH * cols
    depth = w_out.shape[0]
    slices = grad_out.shape[0]
    group = lat_size * lon_size
    lat, lon, chan = lax.axis_index("lat"), lax.axis_index("lon"), lax.axis_index("chan")
    me = lat * lon_size + lon
    source_chan = me // slices
    mesh_id = pl.DeviceIdType.MESH

    def remote(src, dst, send, recv, where):
        return pltpu.make_async_remote_copy(
            src_ref=src,
            dst_ref=dst,
            send_sem=send,
            recv_sem=recv,
            device_id=where,
            device_id_type=mesh_id,
        )

    def place(index):
        return index // lon_size, lax.rem(index, lon_size)

    total_devices = group * chan_size
    mine = me * chan_size + chan
    barrier = pltpu.get_barrier_semaphore()

    def greet(step, carry):
        other = lax.rem(mine + step, total_devices)
        to_lat, to_lon = place(other // chan_size)
        pl.semaphore_signal(
            barrier,
            inc=1,
            device_id=(to_lat, to_lon, lax.rem(other, chan_size)),
            device_id_type=mesh_id,
        )
        return carry

    lax.fori_loop(1, total_devices, greet, 0)
    own_copies = [
        pltpu.make_async_copy(x, kv.at[i, 0, pl.ds(rim, tokens)], own_sem.at[i])
        for i, x in enumerate((keys, values))
    ]
    own_at = pl.ds(pl.multiple_of(me * tokens, tokens), tokens)
    own_copies.append(pltpu.make_async_copy(attn, saved.at[own_at], own_sem.at[2]))
    for copy in own_copies:
        copy.start()
    pl.semaphore_wait(barrier, total_devices - 1)

    def block_at(index):
        return pl.ds(pl.multiple_of(index * tokens, tokens), tokens)

    def feature_copy(i, j):
        target = chan * slices + i
        to_lat, to_lon = place(target)
        to_chan, away = chan, target != me
        src, dst = grad_out.at[i], feat.at[block_at(me)]
        out = remote(
            src, dst, feat_out_sem.at[i, j], feat_sem.at[me], (to_lat, to_lon, to_chan)
        )
        return away, out, (src, dst, feat_sem.at[me])

    for i in range(slices):
        for j in range(1):
            away, out, own = feature_copy(i, j)
            pl.when(away)(out.start)
            pl.when(jnp.logical_not(away))(lambda own=own: pltpu.make_async_copy(*own).start())

    def rim_pieces():
        pieces = []
        for b in range(blocks):
            to_lon = lax.rem(lon + (0, lon_size - 1, 1)[b], lon_size)
            from_lon = lax.rem(lon + (0, 1, lon_size - 1)[b], lon_size)
            for d, (shift, own, ext) in enumerate(
                (
                    (0, (0, tokens), (rim, tokens)),
                    (1, (tokens - rim, rim), (0, rim)),
                    (-1, (0, rim), (rim + tokens, rim)),
                )
            ):
                if b or d:
                    pieces.append((b, d, shift, own, ext, to_lon, from_lon))
        return pieces

    def inside(shift):
        return (lat + shift >= 0) & (lat + shift < lat_size)

    def kv_copy(piece, i):
        b, d, shift, own, ext, to_lon, _ = piece
        return remote(
            (keys, values)[i].at[pl.ds(*own)],
            kv.at[i, b, pl.ds(*ext)],
            kv_out_sem.at[i, b, d],
            kv_sem.at[i, b, d],
            (lat + shift, to_lon, chan),
        )

    for piece in rim_pieces():
        for i in range(2):
            pl.when(inside(piece[2]))(kv_copy(piece, i).start)

    last = 2 * rim + tokens
    for i in range(2):
        for b in range(blocks):
            if span > last:
                kv[i, b, pl.ds(last, span - last), :] = jnp.zeros((span - last, width), BF16)

            @pl.when(lat == 0)
            def _():
                kv[i, b, pl.ds(0, rim), :] = jnp.zeros((rim, width), BF16)

            @pl.when(lat == lat_size - 1)
            def _():
                kv[i, b, pl.ds(rim + tokens, rim), :] = jnp.zeros((rim, width), BF16)

    lat_first = lat * rows
    def saved_copy(to_lat, slot):
        return remote(
            attn,
            saved.at[block_at(slot)],
            saved_out_sem.at[to_lat],
            saved_sem.at[slot],
            (to_lat, lon, chan),
        )

    def saved_pass(row_block, to_lon):
        index = row_block * lon_size + lon
        src = saved.at[block_at(index)]
        return remote(
            src, src, saved_on_sem.at[row_block, to_lon], saved_sem.at[index], (lat, to_lon, chan)
        )

    def saved_arrival(index):
        at = saved.at[block_at(index)]
        return remote(at, at, saved_out_sem.at[0], saved_sem.at[index], (lat, lon, chan))

    primary = lax.rem(source_chan, 2) == lax.rem(chan, 2)
    def start_saved(step, carry):
        saved_copy(lax.rem(lat + step, lat_size), me).start()
        return carry

    lax.fori_loop(1, lat_size, start_saved, 0)

    def relay_copy(index, j):
        at = feat.at[block_at(index)]
        to_chan = lax.rem(chan + 2 * j, chan_size)
        return remote(at, at, relay_sem.at[index, j], feat_sem.at[index], (lat, lon, to_chan))

    def pass_copy(index):
        sibling = chan + 1 - 2 * lax.rem(chan, 2)
        at = feat.at[block_at(index)]
        return remote(at, at, pass_sem.at[index], feat_sem.at[index], (lat, lon, sibling))

    def part_copy(index):
        to_lat, to_lon = place(index)
        return remote(
            part.at[block_at(index)],
            side.at[lon, to_lat],
            part_out_sem.at[index],
            side_sem.at[lon, to_lat],
            (lat, to_lon, chan),
        )

    def side_arrival(from_lon, row_block):
        return remote(
            side.at[from_lon, row_block],
            side.at[from_lon, row_block],
            part_out_sem.at[0],
            side_sem.at[from_lon, row_block],
            (lat, from_lon, chan),
        )

    def back_copy(row_block, slot):
        return remote(
            ready.at[row_block],
            back.at[slot],
            back_out_sem.at[row_block],
            back_sem.at[slot],
            (row_block, lon, chan),
        )

    def one_block(step, carry):
        at_lat = lax.rem(lat + 1 + step // lon_size, lat_size)
        at_lon = lax.rem(lon + 1 + lax.rem(step, lon_size), lon_size)
        index = at_lat * lon_size + at_lon
        at = feat.at[block_at(index)]
        is_own = (index == me) & (source_chan == chan)
        local_copy = pltpu.make_async_copy(grad_out.at[0], at, feat_sem.at[index])
        arrival = remote(at, at, pass_sem.at[index], feat_sem.at[index], (lat, lon, chan))
        pl.when(is_own)(local_copy.wait)
        pl.when(jnp.logical_not(is_own))(arrival.wait_recv)
        pl.when(primary)(pass_copy(index).start)
        for j in range(1, chan_size // 2):
            pl.when(source_chan == chan)(relay_copy(index, j).start)
        product = jnp.dot(
            feat[block_at(index), :], w_out[...], preferred_element_type=F32
        )

        part[block_at(index), :] = product.astype(BF16)

        @pl.when(at_lon == lon)
        def _():
            own_part[at_lat] = product

        @pl.when(at_lon != lon)
        def _():
            part_copy(index).start()

        return carry

    lax.fori_loop(0, group, one_block, 0)

    def one_sum(step, carry):
        row_block = lax.rem(lat + step, lat_size)

        def add_side(turn, total):
            from_lon = lax.rem(lon + turn, lon_size)
            side_arrival(from_lon, row_block).wait_recv()
            return total + side[from_lon, row_block].astype(F32)

        total = lax.fori_loop(1, lon_size, add_side, own_part[row_block])
        own_part[row_block] = total

        @pl.when(row_block != lat)
        def _():
            ready[row_block] = total.astype(BF16)
            back_copy(row_block, lat).start()

        return carry

    lax.fori_loop(1, lat_size + 1, one_sum, 0)
    for copy in own_copies:
        copy.wait()
    def pass_saved(step, carry):
        row_block = lax.rem(lat + step, lat_size)

        @pl.when(step > 0)
        def _():
            saved_arrival(row_block * lon_size + lon).wait_recv()

        def to_side(turn, carry):
            saved_pass(row_block, lax.rem(lon + turn, lon_size)).start()
            return carry

        return lax.fori_loop(1, lon_size, to_side, carry)

    lax.fori_loop(0, lat_size, pass_saved, 0)


    allowed = allowed_pairs(
        valid[...], lat_first, lat_size * rows, rows, cols, slots, blocks, lon_size
    )
    spread = expand_bias(diag[...], cols, slots)
    for piece in rim_pieces():
        for i in range(2):
            pl.when(inside(-piece[2]))(kv_copy(piece, i).wait_recv)

    def add_block(step, total):
        row_block = lax.rem(lat + step, lat_size)
        back_copy(row_block, row_block).wait_recv()
        return total + back[row_block].astype(F32)

    grad_attn[...] = lax.fori_loop(1, lat_size, add_block, own_part[lat]).astype(BF16)

    for h in range(heads):
        at = pl.ds(h * HEAD_DIM, HEAD_DIM)
        head_bias = spread[h * blocks * cols : (h + 1) * blocks * cols]
        grad_q, grad_k, grad_v, folded = attend(
            dims,
            allowed,
            head_bias,
            q[:, at],
            grad_attn[:, at],
            kv[0, :, :, at].reshape(blocks * span, HEAD_DIM),
            kv[1, :, :, at].reshape(blocks * span, HEAD_DIM),
        )
        gq[:, at] = grad_q.astype(BF16)
        for i, grad in enumerate((grad_k, grad_v)):
            gkv[i, :, at] = grad[rim : rim + tokens]
            gsend[i, :, :, at] = grad.astype(BF16).reshape(blocks, span, HEAD_DIM)
        for b in range(blocks):
            fold[pl.ds((h * blocks + b) * cols, cols), :] = folded[b]

    def grad_copy(piece, i):
        b, d, shift, _, ext, _, from_lon = piece
        dst = gmid.at[i, b] if d == 0 else grim.at[i, b, d - 1]
        return remote(
            gsend.at[i, b, pl.ds(*ext)],
            dst,
            g_out_sem.at[i, b, d],
            g_sem.at[i, b, d],
            (lat - shift, from_lon, chan),
        )

    for piece in rim_pieces():
        for i in range(2):
            pl.when(inside(-piece[2]))(grad_copy(piece, i).start)

    tables[me] = collapse_bias(fold[...], cols, slots)

    def table_copy(index, slot):
        to_lat, to_lon = place(index)
        return remote(
            tables.at[me],
            tables.at[slot],
            t_out_sem.at[index],
            t_sem.at[slot],
            (to_lat, to_lon, chan),
        )

    def start_table(step, carry):
        table_copy(lax.rem(me + step, group), me).start()
        return carry

    lax.fori_loop(1, group, start_table, 0)


    for i in range(2):
        for piece in rim_pieces():
            b, d, shift, own, *_ = piece

            @pl.when(inside(shift))
            def _():
                grad_copy(piece, i).wait_recv()
                part_in = gmid[i, b] if d == 0 else grim[i, b, d - 1]
                gkv[i, pl.ds(*own), :] = gkv[i, pl.ds(*own), :] + part_in.astype(F32)

        (gk, gv)[i][...] = gkv[i].astype(BF16)

    def add_table(step, total):
        index = lax.rem(me + step, group)
        table_copy(index, index).wait_recv()
        return total + tables[index]

    table[...] = lax.fori_loop(1, group, add_table, tables[me])

    def await_saved(step, carry):
        row_block, turn = step // (lon_size - 1), lax.rem(step, lon_size - 1)
        from_lon = lax.rem(lon + 1 + turn, lon_size)
        saved_arrival(row_block * lon_size + from_lon).wait_recv()
        return carry

    if lon_size > 1:
        lax.fori_loop(0, lat_size * (lon_size - 1), await_saved, 0)
    strip = 128 if width % 128 == 0 else width
    for start in range(0, width, strip):
        wout[:, pl.ds(start, strip)] = lax.dot_general(
            feat[...],
            saved[:, pl.ds(start, strip)],
            (((0,), (0,)), ((), ())),
            preferred_element_type=F32,
        )

    for i in range(slices):
        for j in range(1):
            away, out, _ = feature_copy(i, j)
            pl.when(away)(out.wait_send)
    for piece in rim_pieces():
        for i in range(2):
            pl.when(inside(piece[2]))(kv_copy(piece, i).wait_send)
            pl.when(inside(-piece[2]))(grad_copy(piece, i).wait_send)

    def sent(step, carry):
        index = lax.rem(me + step, group)
        pl.when(primary)(pass_copy(index).wait_send)
        for j in range(1, chan_size // 2):
            pl.when(source_chan == chan)(relay_copy(index, j).wait_send)

        _, at_lon = place(index)

        @pl.when(at_lon != lon)
        def _():
            part_copy(index).wait_send()
            saved_pass(index // lon_size, at_lon).wait_send()

        @pl.when(step > 0)
        def _():
            table_copy(index, me).wait_send()

        return carry

    lax.fori_loop(0, group, sent, 0)

    def sent_rows(step, carry):
        row_block = lax.rem(lat + step, lat_size)
        back_copy(row_block, lat).wait_send()
        saved_copy(row_block, me).wait_send()
        return carry

    lax.fori_loop(1, lat_size, sent_rows, 0)


def diag_table(table, cols, slots, blocks, lon_size):
    heads, height, width = table.shape

    def placed(part, first):
        return jnp.pad(part, ((0, 0), (0, 0), (first, 2 * cols - first - part.shape[2])))

    own = placed(table, cols - 1 - REACH)
    right = placed(table[:, :, REACH + 1 :], 0) if blocks > 1 else None
    left = placed(table[:, :, :REACH], 2 * cols - 1 - REACH) if blocks > 1 else None
    parts = [own] if blocks == 1 else [own, right + left] if lon_size == 2 else [own, right, left]
    stacked = jnp.stack(parts, axis=1)
    stacked = jnp.pad(stacked, ((0, 0), (0, 0), (0, slots - height), (0, 0)))
    return stacked.reshape(heads * blocks, slots * 2 * cols)


def undiag_table(diag, heads, cols, slots, blocks, lon_size):
    grid = diag.reshape(heads, blocks, slots, 2 * cols)[:, :, : 2 * WIN - 1]
    first = cols - 1 - REACH
    own = grid[:, 0, :, first : first + WIN]
    if blocks == 1:
        return own
    right = grid[:, 1, :, :REACH]
    left = grid[:, blocks - 1, :, 2 * cols - 1 - REACH : 2 * cols - 1]
    gap = jnp.zeros(own.shape[:2] + (1,), own.dtype)
    return own + jnp.concatenate([left, gap, right], axis=2)


def valid_row(key_mask, rows, cols, slots, blocks, lon_size):
    lat_total, lon_total = key_mask.shape
    mark = (jnp.arange(lat_total) % 4 == 0)[:, None] & (jnp.arange(lon_total) % 4 == 0)[None, :]
    valid = ((key_mask == 1) | mark).astype(jnp.int32)
    valid = jnp.pad(valid, ((REACH, slots), (0, 0)))
    valid = lax.dynamic_slice_in_dim(valid, lax.axis_index("lat") * rows, slots, 0)
    me = lax.axis_index("lon")
    parts = [
        lax.dynamic_slice_in_dim(valid, (me + step) % lon_size * cols, cols, 1)
        for step in (0, 1, lon_size - 1)[:blocks]
    ]
    return jnp.stack(parts, axis=0).reshape(1, blocks * slots * cols)


def local(queries, keys, values, attn_out, grad_out, w_out, bias_table, key_mask):
    rows, cols, width = queries.shape
    heads = bias_table.shape[0]
    tokens = rows * cols
    lat_size, lon_size = lax.axis_size("lat"), lax.axis_size("lon")
    blocks = min(3, lon_size)
    slots = row_slots(rows, cols)
    span = slots * cols
    rim = REACH * cols
    group = ("lat", "lon")
    dims = (rows, cols, slots, blocks)
    depth = w_out.shape[0]
    sizes = (lat_size, lon_size, lax.axis_size("chan"))
    count = lat_size * lon_size
    slices = grad_out.reshape(tokens, -1, depth).transpose(1, 0, 2)
    diag = diag_table(bias_table, cols, slots, blocks, lon_size)
    valid = valid_row(key_mask, rows, cols, slots, blocks, lon_size)
    vmem = pl.BlockSpec(memory_space=pltpu.VMEM)
    dma = pltpu.SemaphoreType.DMA
    token = jax.ShapeDtypeStruct((tokens, width), BF16)
    table_shape = (heads * blocks, slots * 2 * cols)
    grad_queries, grad_keys, grad_values, diag_grad, grad_wout = pl.pallas_call(
        functools.partial(mega_kernel, dims, sizes),
        out_shape=(
            token,
            token,
            token,
            jax.ShapeDtypeStruct(table_shape, F32),
            jax.ShapeDtypeStruct((depth, width), F32),
        ),
        in_specs=[vmem] * 8,
        out_specs=(vmem,) * 5,
        scratch_shapes=[
            pltpu.VMEM((2, blocks, span, width), BF16),
            pltpu.VMEM((count * tokens, depth), BF16),
            pltpu.VMEM((count * tokens, width), BF16),
            pltpu.VMEM((lon_size, lat_size, tokens, width), BF16),
            pltpu.VMEM((lat_size, tokens, width), BF16),
            pltpu.VMEM((lat_size, tokens, width), F32),
            pltpu.VMEM((lat_size, tokens, width), BF16),
            pltpu.VMEM((count * tokens, width), BF16),
            pltpu.VMEM((tokens, width), BF16),
            pltpu.VMEM((2, tokens, width), F32),
            pltpu.VMEM((2, blocks, span, width), BF16),
            pltpu.VMEM((2, blocks, tokens, width), BF16),
            pltpu.VMEM((2, blocks, 2, rim, width), BF16),
            pltpu.VMEM((heads * blocks * cols, span), F32),
            pltpu.VMEM((count,) + table_shape, F32),
            dma((slices.shape[0], sizes[2] // 2)),
            dma((count,)),
            dma((count,)),
            dma((count, sizes[2] // 2)),
            dma((count,)),
            dma((lon_size, lat_size)),
            dma((lat_size,)),
            dma((lat_size,)),
            dma((lat_size,)),
            dma((lat_size, lon_size)),
            dma((count,)),
            dma((2, blocks, 3)),
            dma((2, blocks, 3)),
            dma((2, blocks, 3)),
            dma((2, blocks, 3)),
            dma((count,)),
            dma((count,)),
            dma((3,)),
        ],
        compiler_params=pltpu.CompilerParams(
            collective_id=0, has_side_effects=True, vmem_limit_bytes=56 * 1024 * 1024
        ),
    )(
        valid,
        diag,
        queries.reshape(tokens, width),
        keys.reshape(tokens, width),
        values.reshape(tokens, width),
        attn_out.reshape(tokens, width),
        slices,
        w_out,
    )
    grad_table = undiag_table(diag_grad, heads, cols, slots, blocks, lon_size)
    tokens_out = [x.reshape(rows, cols, width) for x in (grad_queries, grad_keys, grad_values)]
    return (*tokens_out, grad_wout, grad_table)


def solution(mesh):
    token = P("lat", "lon", "chan")
    matrix = P(("lat", "lon"), "chan")
    table = P("chan", None, None)
    return jax.shard_map(
        local,
        mesh=mesh,
        in_specs=(token, token, token, token, token, matrix, table, P()),
        out_specs=(token, token, token, matrix, table),
        check_vma=False,
    )
```
